32 devices in a mesh: grp: 2 (over y), tok: 8 (over z, x), head: 2 (over core).
Axes of the slice: x: 2, y: 2, z: 4, core: 2. Of those that a mesh axis runs over, the one named last changes fastest.
Arguments:
- events: bfloat16 [16384, 1024], P(('grp', 'tok')), parts along dimension 0, may hold values from -6 to 6
- uvqk_weight: bfloat16 [1024, 4, 1024], P(None, None, 'head'), may hold values from -0.1875 to 0.1875
- out_weight: bfloat16 [1024, 1024], P('head'), may hold values from -0.1875 to 0.1875
- segments: int32 [16, 1024], P(('grp', 'tok')), parts along dimension 0, may hold values from 0 to 7, never falling along the last dimension, each value on 1 to 512 neighbouring positions
Outputs:
- targets: bfloat16 [16384, 1024], P(('grp', 'tok'), 'head'), parts along dimension 0
The draws below stay inside these ranges and needn't reach their ends.
There are 2 independent parts, one for each index of `grp`. The reference program is written for one: setup_inputs(seed, part) draws one part's arguments, and reference() takes and returns one part's arrays. A program takes and returns all parts, laid end to end along the dimension named above; an argument that names none is the same for every part. Nothing has to cross between parts.
Inputs may be any that keep to these rules, and one draw needn't show every extreme that they name: `segments`: in each row numbers never fall; every user 0 to 7 holds 1 to 512 consecutive rows of its owner, and some user holds exactly 512.
All inputs are finite; a program needn't handle non-finite values.
Results may differ from the reference program's by a relative error of at most 0.007.
Values may be sent and summed in bfloat16 or wider, within the bound.
A program may use at most 64 MiB of HBM per device.

```python
import math
import jax
import jax.numpy as jnp
import numpy as np
from jax import lax

D = 1024
HD = 128
TOK_DEV = 1024
USERS_OWN = 8
BLK = 128
MAXLEN = 512
SLOT = 128
TOKENS = 8192
HGRP = 2
N_TOK = 8


def block_levels(stream_key, dims, split, low, top_value):
    loudness = 1.0
    for dim, blocks in split:
        heights = jax.random.uniform(jax.random.fold_in(jax.random.fold_in(stream_key, 6), dim), (blocks,), jnp.float32, low / len(split), top_value / len(split))
        loudness = loudness * jnp.repeat(jnp.exp(heights), dims[dim] // blocks).reshape((-1,) + (1,) * (len(dims) - 1 - dim))
    return loudness


def profile(number_of, total, limit, lean):
    loads = [(1 << 20) // math.isqrt(rank ** lean) + 1 for rank in range(2, number_of + 1)]
    rest, holding = total - limit - (number_of - 1), [1] * (number_of - 1)
    while rest > 0:
        candidates = [i for i in range(number_of - 1) if holding[i] < limit]
        pool, remaining = sum([loads[i] for i in candidates]), rest
        for i in candidates:
            extra = min(limit - holding[i], max(1, remaining * loads[i] // pool), rest)
            holding[i] = holding[i] + extra
            rest = rest - extra
    return np.array([limit] + holding)


def ragged(key, amount, total, most, lean):
    if amount == 2:
        one = jax.random.randint(key, (), max(1, total - most), min(most, total - 1) + 1)
        return jnp.stack([one, total - one])
    sizes = jnp.asarray(profile(amount, total, most, lean), jnp.int32)
    twos = (amount - 1) // 2
    donor, receiver = sizes[1:1 + 2 * twos:2], sizes[2:2 + 2 * twos:2]
    room = jnp.minimum(donor - 1, most - receiver)
    moved = jax.random.randint(jax.random.fold_in(key, 1), (twos,), 0, 1 << 20) % (room + 1)
    sizes = sizes.at[1:1 + 2 * twos:2].set(donor - moved).at[2:2 + 2 * twos:2].set(receiver + moved)
    return sizes[jax.random.permutation(jax.random.fold_in(key, 2), amount)]


def scatter_about(rng, extent, deviation, reach, split=(), kind=jnp.bfloat16):
    array = deviation * jax.random.normal(rng, extent, jnp.float32)
    if split:
        array = array * block_levels(rng, extent, split, -0.22, 0.18)
    return jnp.clip(array, -reach, reach).astype(kind)


def setup_inputs(seed: int = 0, part: int = 0) -> dict:
    seeds = jax.random.split(jax.random.key(seed), 5)
    own_keys = jax.random.split(jax.random.fold_in(seeds[4], part), 5)
    events = scatter_about(own_keys[0], (TOKENS, D), 1.0, 6.0, ((0, 8),))
    uvqk_weight = scatter_about(seeds[1], (D, 4, D), D ** -0.5, 0.1875, ((2, 2),))
    out_weight = scatter_about(seeds[2], (D, D), D ** -0.5, 0.1875, ((0, 2),))
    segments = jax.vmap(lambda own: jnp.searchsorted(jnp.cumsum(ragged(own, USERS_OWN, TOK_DEV, MAXLEN, 2)), jnp.arange(TOK_DEV), side="right"))(jax.random.split(own_keys[3], N_TOK)).reshape((N_TOK, TOK_DEV)).astype(jnp.int32)
    return {"events": events, "uvqk_weight": uvqk_weight, "out_weight": out_weight, "segments": segments}


def project(features, uvqk_weight):
    mixed_rows = jnp.einsum('td,dkf->tkf', features.astype(jnp.float32), uvqk_weight.astype(jnp.float32))
    rounded = jax.nn.silu(mixed_rows).astype(jnp.bfloat16)
    return lax.optimization_barrier(rounded)

def positions(segments, user_count):
    user_ids = jnp.arange(user_count, dtype=jnp.int32)
    member = (segments[:, None] == user_ids[None, :]).astype(jnp.int32)
    counts = lax.optimization_barrier(jnp.sum(member, axis=0))
    firsts = jnp.cumsum(counts) - counts
    first_row = lax.optimization_barrier(jnp.sum(member * firsts[None, :], axis=1))
    return jnp.arange(segments.shape[0], dtype=jnp.int32) - first_row

def attend(uvqk_rows, segments):
    row_count = uvqk_rows.shape[0]
    heads_here = uvqk_rows.shape[2] // HD
    split_rows = uvqk_rows.reshape(row_count, 4, heads_here, HD)
    gate_rows = split_rows[:, 0]
    value_rows = split_rows[:, 1].astype(jnp.float32)
    query_rows = split_rows[:, 2]
    key_rows = split_rows[:, 3].astype(jnp.float32)
    blocks = positions(segments, USERS_OWN) // BLK
    qblock = min(512, row_count)
    block_count = row_count // qblock

    def one_block(block_index):
        begin_row = block_index * qblock
        query_part = lax.dynamic_slice_in_dim(query_rows, begin_row, qblock, 0).astype(jnp.float32)
        gate_part = lax.dynamic_slice_in_dim(gate_rows, begin_row, qblock, 0).astype(jnp.float32)
        seg_part = lax.dynamic_slice_in_dim(segments, begin_row, qblock, 0)
        blk_part = lax.dynamic_slice_in_dim(blocks, begin_row, qblock, 0)
        scores = jnp.einsum('qhe,khe->hqk', query_part, key_rows) * HD ** (-0.5)
        allowed = (seg_part[:, None] == segments[None, :]) & (blocks[None, :] <= blk_part[:, None])
        weights = jnp.where(allowed[None], jax.nn.silu(scores), 0.0).astype(jnp.bfloat16)
        weights = lax.optimization_barrier(weights).astype(jnp.float32)
        mixed_rows = jnp.einsum('hqk,khe->qhe', weights, value_rows)
        normed = mixed_rows * lax.rsqrt(lax.optimization_barrier(jnp.mean(mixed_rows * mixed_rows, axis=-1, keepdims=True)) + 1e-06)
        return (normed * gate_part).astype(jnp.bfloat16).reshape(qblock, heads_here * HD)
    outputs = lax.map(one_block, jnp.arange(block_count, dtype=jnp.int32))
    return outputs.reshape(row_count, heads_here * HD)

def reference(events, uvqk_weight, out_weight, segments):
    grid = events.reshape(N_TOK, N_TOK, SLOT, D)
    group_width = D // HGRP

    def per_owner(owner_index):
        owner_rows = lax.dynamic_index_in_dim(grid, owner_index, 1, keepdims=False).reshape(TOK_DEV, D)
        owner_segments = lax.dynamic_index_in_dim(segments, owner_index, 0, keepdims=False)
        attended = attend(project(owner_rows, uvqk_weight), owner_segments)
        branch = jnp.zeros((TOK_DEV, D), jnp.float32)
        for group in range(HGRP):
            columns = attended[:, group * group_width:(group + 1) * group_width]
            partial_value = jnp.dot(columns, out_weight[group * group_width:(group + 1) * group_width], preferred_element_type=jnp.float32)
            partial_value = lax.optimization_barrier(partial_value.astype(jnp.bfloat16))
            branch = branch + partial_value.astype(jnp.float32)
        return (owner_rows.astype(jnp.float32) + branch).astype(jnp.bfloat16)
    outputs = lax.map(per_owner, jnp.arange(N_TOK, dtype=jnp.int32))
    return outputs.reshape(N_TOK, N_TOK, SLOT, D).transpose(1, 0, 2, 3).reshape(TOKENS, D)
```

```python
import functools

import jax
import jax.numpy as jnp
from jax import lax
from jax.experimental import pallas as pl
from jax.experimental.pallas import tpu as pltpu
from jax.sharding import PartitionSpec as P

HD = 128
USERS_OWN = 8
BLK = 128
MAXLEN = 512
MESH = pl.DeviceIdType.MESH


def half_silu(half):
    return half + half * jnp.tanh(half)


def kernel(
    owners, seg_ref, events, w_hbm, wo_hbm, out,
    xb, wv, wov, uvqk, lo_ref, hi_ref, own_part, prx, ptx, obuf,
    w_sem, wo_sem, loc_sem, in_send, in_recv, fwd_send, fwd_recv,
    pp_send, pp_recv, out_send, out_recv, ol_sem,
):
    grp, me, core = lax.axis_index("grp"), lax.axis_index("tok"), lax.axis_index("head")
    rows, dim = events.shape
    slot = rows // owners
    half = out.shape[1]
    width = wo_hbm.shape[0]
    heads = width // HD
    tiles = rows // BLK
    per_tile = BLK // slot
    mine = pl.ds(pl.multiple_of(core * half, half), half)
    theirs = pl.ds(pl.multiple_of((1 - core) * half, half), half)

    def peer(i):
        if owners & (owners - 1):
            return lax.rem(me + i, owners)
        total, bit = 0, 1
        while bit < owners:
            total = total + ((me // bit + i // bit) % 2) * bit
            bit *= 2
        return total

    def slot_rows(s):
        return pl.ds(pl.multiple_of(s * slot, slot), slot)

    def in_copy(s, d):
        return pltpu.make_async_remote_copy(
            src_ref=events.at[slot_rows(d), mine], dst_ref=xb.at[slot_rows(s), mine],
            send_sem=in_send.at[d], recv_sem=in_recv.at[s],
            device_id=(grp, d, core), device_id_type=MESH)

    def fwd_copy(s, cols):
        return pltpu.make_async_remote_copy(
            src_ref=xb.at[slot_rows(s), cols], dst_ref=xb.at[slot_rows(s), cols],
            send_sem=fwd_send.at[s], recv_sem=fwd_recv.at[s],
            device_id=(grp, me, 1 - core), device_id_type=MESH)

    def pp_copy(t):
        return pltpu.make_async_remote_copy(
            src_ref=ptx.at[pl.ds(t * BLK, BLK)], dst_ref=prx.at[pl.ds(t * BLK, BLK)],
            send_sem=pp_send.at[t], recv_sem=pp_recv.at[t],
            device_id=(grp, me, 1 - core), device_id_type=MESH)

    def out_copy(s, d):
        return pltpu.make_async_remote_copy(
            src_ref=obuf.at[slot_rows(d)], dst_ref=out.at[slot_rows(s)],
            send_sem=out_send.at[d], recv_sem=out_recv.at[s],
            device_id=(grp, d, core), device_id_type=MESH)

    out_local = pltpu.make_async_copy(obuf.at[slot_rows(me)], out.at[slot_rows(me)], ol_sem)
    x_local = pltpu.make_async_copy(events.at[slot_rows(me)], xb.at[slot_rows(me)], loc_sem)
    w_copy = pltpu.make_async_copy(w_hbm, wv, w_sem)
    wo_copy = pltpu.make_async_copy(wo_hbm, wov, wo_sem)

    barrier = pltpu.get_barrier_semaphore()

    @pl.loop(1, owners)
    def _(i):
        pl.semaphore_signal(barrier, inc=1, device_id=(grp, peer(i), core), device_id_type=MESH)

    pl.semaphore_signal(barrier, inc=1, device_id=(grp, me, 1 - core), device_id_type=MESH)
    x_local.start()
    w_copy.start()
    wo_copy.start()
    pl.semaphore_wait(barrier, owners)

    @pl.loop(1, owners)
    def _(i):
        d = peer(owners - i)
        in_copy(me, d).start()

    segr = seg_ref[...]
    seg_t = jnp.transpose(jnp.broadcast_to(segr, (BLK, rows)))
    row = lax.broadcasted_iota(jnp.int32, (rows, BLK), 0)
    starts = [
        jnp.sum((segr < u).astype(jnp.int32), axis=1, keepdims=True) for u in range(USERS_OWN + 1)
    ]
    first = jnp.zeros((rows, BLK), jnp.int32)
    end = jnp.zeros((rows, BLK), jnp.int32)
    for u in range(USERS_OWN):
        here = seg_t == u
        first = jnp.where(here, starts[u], first)
        end = jnp.where(here, starts[u + 1], end)
    blocks = lax.shift_right_logical(row - first, BLK.bit_length() - 1)
    lo_ref[...] = first
    hi_ref[...] = jnp.minimum(end, first + (blocks + 1) * BLK)

    def project(s):
        x = xb[slot_rows(s), :]
        for k in range(4):
            cols = slice(k * width, (k + 1) * width)
            v = jnp.dot(x, wv[:, cols], preferred_element_type=jnp.float32)
            uvqk[slot_rows(s), cols] = half_silu(v * 0.5).astype(jnp.bfloat16)

    x_local.wait()
    w_copy.wait()
    project(me)
    s1 = peer(1)
    in_copy(s1, s1).wait_recv()
    fwd_copy(s1, mine).start()

    @pl.loop(2, owners)
    def _(i):
        s, before = peer(i), peer(i - 1)
        in_copy(s, s).wait_recv()
        fwd_copy(s, mine).start()
        fwd_copy(before, theirs).wait_recv()
        project(before)

    last = peer(owners - 1)
    fwd_copy(last, theirs).wait_recv()
    project(last)
    wo_copy.wait()

    def finish(t):
        pp_copy(t).wait_recv()
        r = pl.ds(t * BLK, BLK)
        total = (
            xb[r, mine].astype(jnp.float32)
            + own_part[r, :].astype(jnp.float32)
            + prx[r, :].astype(jnp.float32)
        )
        obuf[r, :] = total.astype(jnp.bfloat16)
        for p in range(per_tile):
            s = t * per_tile + p

            @pl.when(s == me)
            def _():
                out_local.start()

            @pl.when(s != me)
            def _():
                out_copy(me, s).start()

    scale = 0.5 * HD ** (-0.5)
    reach = MAXLEN // BLK
    for t in range(tiles):
        a, b = max(0, t - reach), min(tiles, t + 2)
        r = slice(t * BLK, (t + 1) * BLK)
        keys = slice(a * BLK, b * BLK)
        span = (b - a) * BLK
        at = lax.broadcasted_iota(jnp.int32, (BLK, span), 1) + a * BLK
        lo = jnp.concatenate([lo_ref[r, :]] * (b - a), axis=1)
        hi = jnp.concatenate([hi_ref[r, :]] * (b - a), axis=1)
        allowed = (at >= lo) & (at < hi)
        columns = []
        for h in range(heads):
            def part(k):
                return slice(k * width + h * HD, k * width + (h + 1) * HD)

            scores = lax.dot_general(
                uvqk[r, part(2)], uvqk[keys, part(3)], (((1,), (1,)), ((), ())),
                preferred_element_type=jnp.float32)
            weights = jnp.where(allowed, half_silu(scores * scale), 0.0).astype(jnp.bfloat16)
            mixed = jnp.dot(weights, uvqk[keys, part(1)], preferred_element_type=jnp.float32)
            normed = mixed * lax.rsqrt(jnp.mean(mixed * mixed, axis=-1, keepdims=True) + 1e-06)
            columns.append((normed * uvqk[r, part(0)].astype(jnp.float32)).astype(jnp.bfloat16))
        att = jnp.concatenate(columns, axis=1)
        ptx[r, :] = jnp.dot(att, wov[:, theirs], preferred_element_type=jnp.float32).astype(jnp.bfloat16)
        pp_copy(t).start()
        own_part[r, :] = jnp.dot(att, wov[:, mine], preferred_element_type=jnp.float32).astype(jnp.bfloat16)
        if t:
            finish(t - 1)
    finish(tiles - 1)

    @pl.loop(1, owners)
    def _(i):
        s = peer(i)
        in_copy(me, s).wait_send()
        fwd_copy(s, mine).wait_send()
        out_copy(me, s).wait_send()
        out_copy(s, s).wait_recv()

    for t in range(tiles):
        pp_copy(t).wait_send()
    out_local.wait()


def per_device(events, uvqk_weight, out_weight, segments):
    owners = lax.axis_size("tok")
    rows, dim = events.shape
    width = uvqk_weight.shape[2]
    half = dim // lax.axis_size("head")
    tiles = rows // BLK
    w2 = uvqk_weight.reshape(dim, 4 * width)
    dma = pltpu.SemaphoreType.DMA
    hbm = pl.BlockSpec(memory_space=pl.ANY)
    bf = jnp.bfloat16
    return pl.pallas_call(
        functools.partial(kernel, owners),
        out_shape=jax.ShapeDtypeStruct((rows, half), bf),
        in_specs=[pl.BlockSpec(memory_space=pltpu.VMEM), hbm, hbm, hbm],
        out_specs=hbm,
        scratch_shapes=[
            pltpu.VMEM((rows, dim), bf),
            pltpu.VMEM((dim, 4 * width), bf),
            pltpu.VMEM((width, dim), bf),
            pltpu.VMEM((rows, 4 * width), bf),
            pltpu.VMEM((rows, BLK), jnp.int32),
            pltpu.VMEM((rows, BLK), jnp.int32),
            pltpu.VMEM((rows, half), bf),
            pltpu.VMEM((rows, half), bf),
            pltpu.VMEM((rows, half), bf),
            pltpu.VMEM((rows, half), bf),
            dma, dma, dma,
            dma((owners,)), dma((owners,)), dma((owners,)), dma((owners,)),
            dma((tiles,)), dma((tiles,)), dma((owners,)), dma((owners,)), dma,
        ],
        compiler_params=pltpu.CompilerParams(
            collective_id=0, has_side_effects=True, vmem_limit_bytes=48 * 2**20
        ),
    )(segments, events, w2, out_weight)


def solution(mesh):
    in_specs = (
        P(("grp", "tok"), None),
        P(None, None, "head"),
        P("head", None),
        P(("grp", "tok"), None),
    )
    return jax.shard_map(
        per_device, mesh=mesh, in_specs=in_specs, out_specs=P(("grp", "tok"), "head"), check_vma=False
    )
```

```python
import functools

import jax
import jax.numpy as jnp
from jax import lax
from jax.experimental import pallas as pl
from jax.experimental.pallas import tpu as pltpu
from jax.sharding import PartitionSpec as P

HD = 128
USERS_OWN = 8
BLK = 128
MAXLEN = 512
MESH = pl.DeviceIdType.MESH


def half_silu(half):
    return half + half * jnp.tanh(half)


def kernel(
    owners, seg_hbm, events, w_hbm, wo_hbm, out,
    seg_ref, xb, w3, wv, wov, uvqk, lo_ref, hi_ref, own_part, prx, ptx, obuf,
    seg_sem, w_sem, wo_sem, loc_sem, in_send, in_recv, fwd_send, fwd_recv,
    pp_send, pp_recv, out_send, out_recv, ol_sem,
):
    grp, me, core = lax.axis_index("grp"), lax.axis_index("tok"), lax.axis_index("head")
    rows, dim = events.shape
    slot = rows // owners
    half = out.shape[1]
    width = wo_hbm.shape[0]
    heads = width // HD
    tiles = rows // BLK
    per_tile = BLK // slot
    mine = pl.ds(pl.multiple_of(core * half, half), half)
    theirs = pl.ds(pl.multiple_of((1 - core) * half, half), half)

    def peer(i):
        if owners & (owners - 1):
            return lax.rem(me + i, owners)
        total, bit = 0, 1
        while bit < owners:
            total = total + ((me // bit + i // bit) % 2) * bit
            bit *= 2
        return total

    def slot_rows(s):
        return pl.ds(pl.multiple_of(s * slot, slot), slot)

    def share(s, c):
        if slot % 32:
            return slot_rows(s), pl.ds(pl.multiple_of(c * half, half), half)
        return pl.ds(pl.multiple_of(s * slot + c * (slot // 2), slot // 2), slot // 2), slice(None)

    def in_copy(s, d):
        return pltpu.make_async_remote_copy(
            src_ref=events.at[share(d, core)], dst_ref=xb.at[share(s, core)],
            send_sem=in_send.at[d], recv_sem=in_recv.at[s],
            device_id=(grp, d, core), device_id_type=MESH)

    def fwd_copy(s, c):
        return pltpu.make_async_remote_copy(
            src_ref=xb.at[share(s, c)], dst_ref=xb.at[share(s, c)],
            send_sem=fwd_send.at[s], recv_sem=fwd_recv.at[s],
            device_id=(grp, me, 1 - core), device_id_type=MESH)

    def pp_copy(t):
        return pltpu.make_async_remote_copy(
            src_ref=ptx.at[pl.ds(t * BLK, BLK)], dst_ref=prx.at[pl.ds(t * BLK, BLK)],
            send_sem=pp_send.at[t], recv_sem=pp_recv.at[t],
            device_id=(grp, me, 1 - core), device_id_type=MESH)

    def out_copy(s, d):
        return pltpu.make_async_remote_copy(
            src_ref=obuf.at[slot_rows(d)], dst_ref=out.at[slot_rows(s)],
            send_sem=out_send.at[d], recv_sem=out_recv.at[s],
            device_id=(grp, d, core), device_id_type=MESH)

    out_local = pltpu.make_async_copy(obuf.at[slot_rows(me)], out.at[slot_rows(me)], ol_sem)
    x_local = pltpu.make_async_copy(events.at[slot_rows(me)], xb.at[slot_rows(me)], loc_sem)
    w_copy = pltpu.make_async_copy(w_hbm, w3, w_sem)
    wo_copy = pltpu.make_async_copy(wo_hbm, wov, wo_sem)

    barrier = pltpu.get_barrier_semaphore()

    @pl.loop(1, owners)
    def _(i):
        pl.semaphore_signal(barrier, inc=1, device_id=(grp, peer(i), core), device_id_type=MESH)

    pl.semaphore_signal(barrier, inc=1, device_id=(grp, me, 1 - core), device_id_type=MESH)
    seg_copy = pltpu.make_async_copy(seg_hbm, seg_ref, seg_sem)
    seg_copy.start()
    x_local.start()
    w_copy.start()
    wo_copy.start()
    pl.semaphore_wait(barrier, owners)

    @pl.loop(1, owners)
    def _(i):
        d = peer(i)
        in_copy(me, d).start()

    seg_copy.wait()
    segr = seg_ref[...]
    seg_t = jnp.transpose(jnp.broadcast_to(segr, (BLK, rows)))
    row = lax.broadcasted_iota(jnp.int32, (rows, BLK), 0)
    starts = [
        jnp.sum((segr < u).astype(jnp.int32), axis=1, keepdims=True) for u in range(USERS_OWN + 1)
    ]
    first = jnp.zeros((rows, BLK), jnp.int32)
    end = jnp.zeros((rows, BLK), jnp.int32)
    for u in range(USERS_OWN):
        here = seg_t == u
        first = jnp.where(here, starts[u], first)
        end = jnp.where(here, starts[u + 1], end)
    blocks = lax.shift_right_logical(row - first, BLK.bit_length() - 1)
    lo_ref[...] = first
    hi_ref[...] = jnp.minimum(end, first + (blocks + 1) * BLK)

    def project(s):
        x = xb[slot_rows(s), :]
        for k in range(4):
            cols = slice(k * width, (k + 1) * width)
            v = jnp.dot(x, wv[:, cols], preferred_element_type=jnp.float32)
            uvqk[slot_rows(s), cols] = half_silu(v * 0.5).astype(jnp.bfloat16)

    def finish(t):
        pp_copy(t).wait_recv()
        r = pl.ds(t * BLK, BLK)
        total = (
            xb[r, mine].astype(jnp.float32)
            + own_part[r, :].astype(jnp.float32)
            + prx[r, :].astype(jnp.float32)
        )
        obuf[r, :] = total.astype(jnp.bfloat16)
        for p in range(per_tile):
            s = t * per_tile + p

            @pl.when(s == me)
            def _():
                out_local.start()

            @pl.when(s != me)
            def _():
                out_copy(me, s).start()

    scale = 0.5 * HD ** (-0.5)
    reach = MAXLEN // BLK
    def attend(t):
        a, b = max(0, t - reach), min(tiles, t + 2)
        r = slice(t * BLK, (t + 1) * BLK)
        keys = slice(a * BLK, b * BLK)
        span = (b - a) * BLK
        at = lax.broadcasted_iota(jnp.int32, (BLK, span), 1) + a * BLK
        lo = jnp.concatenate([lo_ref[r, :]] * (b - a), axis=1)
        hi = jnp.concatenate([hi_ref[r, :]] * (b - a), axis=1)
        allowed = (at >= lo) & (at < hi)
        columns = []
        for h in range(heads):
            def part(k):
                return slice(k * width + h * HD, k * width + (h + 1) * HD)

            scores = lax.dot_general(
                uvqk[r, part(2)], uvqk[keys, part(3)], (((1,), (1,)), ((), ())),
                preferred_element_type=jnp.float32)
            weights = jnp.where(allowed, half_silu(scores * scale), 0.0).astype(jnp.bfloat16)
            mixed = jnp.dot(weights, uvqk[keys, part(1)], preferred_element_type=jnp.float32)
            normed = mixed * lax.rsqrt(jnp.mean(mixed * mixed, axis=-1, keepdims=True) + 1e-06)
            columns.append((normed * uvqk[r, part(0)].astype(jnp.float32)).astype(jnp.bfloat16))
        att = jnp.concatenate(columns, axis=1)
        ptx[r, :] = jnp.dot(att, wov[:, theirs], preferred_element_type=jnp.float32).astype(jnp.bfloat16)
        pp_copy(t).start()
        own_part[r, :] = jnp.dot(att, wov[:, mine], preferred_element_type=jnp.float32).astype(jnp.bfloat16)

    def run(order):
        for n, t in enumerate(order):
            attend(t)
            if n:
                finish(order[n - 1])
        finish(order[-1])

    x_local.wait()
    w_copy.wait()

    @pl.loop(0, dim // BLK)
    def _(i):
        d = pl.ds(pl.multiple_of(i * BLK, BLK), BLK)
        for k in range(4):
            wv[d, k * width:(k + 1) * width] = w3[d, k, :]

    project(me)
    s1 = peer(1)
    in_copy(s1, s1).wait_recv()
    fwd_copy(s1, core).start()

    def step(i):
        s, before = peer(i), peer(i - 1)
        in_copy(s, s).wait_recv()
        fwd_copy(s, core).start()
        fwd_copy(before, 1 - core).wait_recv()
        project(before)

    near = owners // 2
    split = near > 1 and not owners & (owners - 1) and tiles >= 4
    middle = tiles // 2
    if split:
        pl.loop(2, near)(step)
        fwd_copy(peer(near - 1), 1 - core).wait_recv()
        project(peer(near - 1))
        wo_copy.wait()

        @pl.when(me < near)
        def _():
            run(list(range(middle - 1)))

        nxt = peer(near)
        in_copy(nxt, nxt).wait_recv()
        fwd_copy(nxt, core).start()
        pl.loop(near + 1, owners)(step)
    else:
        pl.loop(2, owners)(step)
    last = peer(owners - 1)
    fwd_copy(last, 1 - core).wait_recv()
    project(last)
    if split:
        @pl.when(me < near)
        def _():
            run(list(range(middle, tiles)) + [middle - 1])

        @pl.when(me >= near)
        def _():
            run(list(range(tiles)))
    else:
        wo_copy.wait()
        run(list(range(tiles)))


    @pl.loop(1, owners)
    def _(i):
        s = peer(i)
        in_copy(me, s).wait_send()
        fwd_copy(s, core).wait_send()
        out_copy(me, s).wait_send()
        out_copy(s, s).wait_recv()

    for t in range(tiles):
        pp_copy(t).wait_send()
    out_local.wait()


def per_device(events, uvqk_weight, out_weight, segments):
    owners = lax.axis_size("tok")
    rows, dim = events.shape
    width = uvqk_weight.shape[2]
    half = dim // lax.axis_size("head")
    tiles = rows // BLK
    dma = pltpu.SemaphoreType.DMA
    hbm = pl.BlockSpec(memory_space=pl.ANY)
    bf = jnp.bfloat16
    return pl.pallas_call(
        functools.partial(kernel, owners),
        out_shape=jax.ShapeDtypeStruct((rows, half), bf),
        in_specs=[hbm] * 4,
        out_specs=hbm,
        scratch_shapes=[
            pltpu.VMEM((1, rows), jnp.int32),
            pltpu.VMEM((rows, dim), bf),
            pltpu.VMEM((dim, 4, width), bf),
            pltpu.VMEM((dim, 4 * width), bf),
            pltpu.VMEM((width, dim), bf),
            pltpu.VMEM((rows, 4 * width), bf),
            pltpu.VMEM((rows, BLK), jnp.int32),
            pltpu.VMEM((rows, BLK), jnp.int32),
            pltpu.VMEM((rows, half), bf),
            pltpu.VMEM((rows, half), bf),
            pltpu.VMEM((rows, half), bf),
            pltpu.VMEM((rows, half), bf),
            dma, dma, dma, dma,
            dma((owners,)), dma((owners,)), dma((owners,)), dma((owners,)),
            dma((tiles,)), dma((tiles,)), dma((owners,)), dma((owners,)), dma,
        ],
        compiler_params=pltpu.CompilerParams(
            collective_id=0, has_side_effects=True, vmem_limit_bytes=61 * 2**20
        ),
    )(segments, events, uvqk_weight, out_weight)


def solution(mesh):
    in_specs = (
        P(("grp", "tok"), None),
        P(None, None, "head"),
        P("head", None),
        P(("grp", "tok"), None),
    )
    return jax.shard_map(
        per_device, mesh=mesh, in_specs=in_specs, out_specs=P(("grp", "tok"), "head"), check_vma=False
    )
```
